256 devices in a mesh: dx: 8 (over x, core), dy: 32 (over z, y).
Axes of the slice: x: 4, y: 4, z: 8, core: 2. Of those that a mesh axis runs over, the one named last changes fastest.
Arguments:
- moments: float32 [35, 65536], P(None, ('dx', 'dy')), may hold values from -4 to 4
- positions: float32 [3, 131072, 128], P(None, ('dx', 'dy')), may hold values from -0.5 to 0.5
- masses: float32 [131072, 128], P(('dx', 'dy')), may hold values from 0.004 to 0.04
- counts: int32 [131072], P(('dx', 'dy')), may hold values from 1 to 128
- node_links: int32 [256, 3, 8, 128], P(('dx', 'dy')), may hold values from -1 to 342, as said below
- leaf_links: int32 [256, 3, 8, 128], P(('dx', 'dy')), may hold values from -1 to 511, as said below
- node_local: int32 [256, 3, 2048], P(('dx', 'dy')), may hold values from 0 to 342, as said below
- leaf_local: int32 [256, 3, 128], P(('dx', 'dy')), may hold values from 0 to 511, as said below
Outputs:
- local_exp: float32 [35, 65536], P(None, ('dx', 'dy'))
- forces: float32 [3, 131072, 128], P(None, ('dx', 'dy'))
The draws below stay inside these ranges and needn't reach their ends.
Inputs may be any that keep to these rules, and one draw needn't show every extreme that they name: `node_links`: slot s of column block a of domain p belongs to peer domain a * 32 + s // 4, never p itself. Field 0 is the domain's own node, or -1 for an empty slot; field 1 is the peer's node; field 2 is a node code whose offset has a largest magnitude of 2 or 3. Peers more than 8 domains away from p along the domain order (taken cyclically over all domains) use at most one slot. Every domain fills all 4 slots of peer p + 1 (cyclically). `leaf_links`: slot s of column block a of domain p belongs to peer domain a * 32 + s // 4, never p itself. Field 0 is the domain's own leaf, or -1 for an empty slot; field 1 is the peer's leaf; field 2 is a leaf code other than 13. Only peers p + 1, p - 1, p + 2, p - 2, p + 32 and p - 32 (cyclically over all domains) have used slots. Every domain fills all 4 slots of peer p + 1. `node_local`: Fields: two different nodes of the domain and a node code whose offset has a largest magnitude of 2 or 3. `leaf_local`: Fields: two different leaves of the domain and a leaf code other than 13.
All inputs are finite; a program needn't handle non-finite values.
Results may differ from the reference program's by a relative error of at most 0.0003.
Values sent between devices are 32-bit elements; how exact they have to be, the bound alone decides.
No kernel may reach another device: no remote copies, remote signals or barrier semaphores. Data moves between devices by JAX's collectives and lax.ppermute only.
A program may use at most 64 MiB of HBM per device.

```python
import math
import jax
import jax.numpy as jnp
from jax import lax

NODE_DEV = 256
LEAF_DEV = 512
NCAP = 4
LCAP = 4
NLOC = 2048
LLOC = 128
CELLS = 128
COEFS = 35
SLABS = 8
SUBS = 32
DOMAINS = 256
NODES = 65536
LEAVES = 131072


def multi_indices_drawn():
    listed = []
    for order in range(5):
        for first in range(order, -1, -1):
            for second in range(order - first, -1, -1):
                listed.append((first, second, order - first - second))
    return listed


def order_scales():
    values = []
    for entry in multi_indices_drawn():
        scale = 1.0
        for _ in range(sum(entry)):
            scale = scale * 0.4
        values.append(scale)
    return jnp.array(values, dtype=jnp.float32)


def outer_codes():
    listed = []
    for code in range(343):
        offset = (code // 49 - 3, code // 7 % 7 - 3, code % 7 - 3)
        if max(abs(offset[0]), abs(offset[1]), abs(offset[2])) >= 2:
            listed.append(code)
    return jnp.array(listed, dtype=jnp.int32)


def node_coder(key, shape):
    picked = jax.random.randint(key, shape, 0, 316)
    return outer_codes()[picked]


def leaf_coder(key, shape):
    picked = jax.random.randint(key, shape, 0, 26)
    return picked + (picked >= 13).astype(jnp.int32)


def node_close(distance):
    return distance <= 8


def leaf_close(distance):
    return (distance <= 2) | (distance == SUBS)


def slot_links(key, capacity, items, coder, closeness, far_most):
    keys = jax.random.split(key, 5)
    level = jax.random.randint(keys[0], (DOMAINS, 1, 1), 1, capacity + 1)
    filled = jnp.minimum(jax.random.randint(keys[1], (DOMAINS, SLABS, SUBS), 0, capacity + 1), level)
    holder = jnp.arange(DOMAINS, dtype=jnp.int32)[:, None, None]
    peer = (jnp.arange(SLABS, dtype=jnp.int32)[:, None] * SUBS + jnp.arange(SUBS, dtype=jnp.int32)[None, :])[None]
    ahead = (peer - holder) % DOMAINS
    distance = jnp.minimum(ahead, DOMAINS - ahead)
    filled = jnp.where(closeness(distance), filled, jnp.minimum(filled, far_most))
    filled = jnp.where(peer == (holder + 1) % DOMAINS, capacity, filled)
    filled = jnp.where(peer == holder, 0, filled)
    slot_number = jnp.arange(capacity, dtype=jnp.int32)
    active = slot_number[None, None, None, :] < filled[:, :, :, None]
    shape = (DOMAINS, SLABS, SUBS, capacity)
    owned = jnp.where(active, jax.random.randint(keys[2], shape, 0, items), -1)
    partner = jax.random.randint(keys[3], shape, 0, items)
    offset = coder(keys[4], shape)
    stacked = jnp.stack([owned, partner, offset], axis=1)
    return stacked.reshape(DOMAINS, 3, SLABS, SUBS * capacity).astype(jnp.int32)


def inner_pairs(key, items, count, coder):
    keys = jax.random.split(key, 3)
    first = jax.random.randint(keys[0], (DOMAINS, count), 0, items)
    second = (first + jax.random.randint(keys[1], (DOMAINS, count), 1, items)) % items
    offset = coder(keys[2], (DOMAINS, count))
    return jnp.stack([first, second, offset], axis=1).astype(jnp.int32)


def draw_moments(key, part):
    key = jax.random.fold_in(key, 11)
    values = jnp.clip(jax.random.normal(key, (COEFS, NODES), jnp.float32), -4.0, 4.0)
    return values * order_scales()[:, None]


def draw_node_links(key, part):
    key = jax.random.fold_in(key, 23)
    return slot_links(key, NCAP, NODE_DEV, node_coder, node_close, 1)


def draw_leaf_links(key, part):
    key = jax.random.fold_in(key, 37)
    return slot_links(key, LCAP, LEAF_DEV, leaf_coder, leaf_close, 0)


def draw_node_local(key, part):
    key = jax.random.fold_in(key, 41)
    return inner_pairs(key, NODE_DEV, NLOC, node_coder)


def draw_leaf_local(key, part):
    key = jax.random.fold_in(key, 53)
    return inner_pairs(key, LEAF_DEV, LLOC, leaf_coder)


def place_ends(drawn, rng, smallest, high):
    shape = drawn.shape
    spot = [jax.random.randint(jax.random.fold_in(rng, axis), (), 0, shape[axis]) for axis in range(len(shape))]
    drawn = drawn.at[tuple(spot)].set(smallest)
    longest = shape.index(max(shape))
    spot[longest] = (spot[longest] + 1) % shape[longest]
    return drawn.at[tuple(spot)].set(high)


def steps_of(key, extent, shards, least, top_value):
    def one(dim, blocks):
        heights = jax.random.uniform(jax.random.fold_in(jax.random.fold_in(key, 6), dim), (blocks,), jnp.float32, least / len(shards), top_value / len(shards))
        return jnp.repeat(jnp.exp(heights), extent[dim] // blocks).reshape((-1,) + (1,) * (len(extent) - dim - 1))

    factor_of = one(*shards[0])
    for cut in shards[1:]:
        factor_of = factor_of * one(*cut)
    return factor_of


def setup_inputs(seed: int = 0) -> dict:
    splits = jax.random.split(jax.random.key(seed), 9)
    return {
        "moments": draw_moments(jax.random.fold_in(splits[8], 71), 0),
        "positions": jnp.clip(jax.random.uniform(splits[1], (3, LEAVES, CELLS), jnp.float32, -0.5, 0.5) * steps_of(splits[1], (3, LEAVES, CELLS), ((1, 256),), -0.4, 0.0), -0.5, 0.5),
        "masses": jnp.clip(jnp.exp(math.log(0.04) - 2.30258502 * jax.random.uniform(splits[2], (LEAVES, CELLS), jnp.float32) ** steps_of(splits[2], (LEAVES, CELLS), ((0, 256),), -0.2, 0.2)), 0.004, 0.04),
        "counts": place_ends(jax.random.randint(splits[3], (LEAVES,), 1, CELLS + 1), jax.random.fold_in(splits[3], 1), 1, CELLS).astype(jnp.int32),
        "node_links": draw_node_links(jax.random.fold_in(splits[8], 71), 0),
        "leaf_links": draw_leaf_links(jax.random.fold_in(splits[8], 71), 0),
        "node_local": draw_node_local(jax.random.fold_in(splits[8], 71), 0),
        "leaf_local": draw_leaf_local(jax.random.fold_in(splits[8], 71), 0),
    }


softening = 0.04

def multi_indices():
    listed = []
    for order in range(5):
        for first in range(order, -1, -1):
            for second in range(order - first, -1, -1):
                listed.append((first, second, order - first - second))
    return listed

def shift_table():
    listed = multi_indices()
    position_of = {entry: number for number, entry in enumerate(listed)}
    rows = []
    for left in listed:
        for right in listed:
            joined = (left[0] + right[0], left[1] + right[1], left[2] + right[2])
            row = [0.0] * len(listed)
            if sum(joined) <= 4:
                row[position_of[joined]] = 1.0
            rows.append(row)
    return jnp.array(rows, dtype=jnp.float32)

def order_signs():
    return jnp.array([1.0 if sum(entry) % 2 == 0 else -1.0 for entry in multi_indices()], dtype=jnp.float32)

def derivatives(sep_x, sep_y, sep_z):
    inverse = 1.0 / jnp.sqrt(sep_x * sep_x + sep_y * sep_y + sep_z * sep_z)
    inverse_sq = inverse * inverse
    terms = {}
    power = inverse
    factor = 1.0
    for level in range(5):
        terms[0, 0, 0, level] = factor * power
        power = power * inverse_sq
        factor = factor * -(2 * level + 1)
    for order in range(1, 5):
        for entry in multi_indices():
            if sum(entry) != order:
                continue
            first, second, third = entry
            for level in range(5 - order):
                if first > 0:
                    value = sep_x * terms[first - 1, second, third, level + 1]
                    if first > 1:
                        value = value + (first - 1) * terms[first - 2, second, third, level + 1]
                elif second > 0:
                    value = sep_y * terms[first, second - 1, third, level + 1]
                    if second > 1:
                        value = value + (second - 1) * terms[first, second - 2, third, level + 1]
                else:
                    value = sep_z * terms[first, second, third - 1, level + 1]
                    if third > 1:
                        value = value + (third - 1) * terms[first, second, third - 2, level + 1]
                terms[first, second, third, level] = value
    return jnp.stack([terms[entry[0], entry[1], entry[2], 0] for entry in multi_indices()])

def node_tile(near_moments, far_moments, codes, lives):
    sep_x = (codes // 49 - 3).astype(jnp.float32)
    sep_y = (codes // 7 % 7 - 3).astype(jnp.float32)
    sep_z = (codes % 7 - 3).astype(jnp.float32)
    deriv = derivatives(sep_x, sep_y, sep_z)
    count = len(multi_indices())
    spread = jnp.dot(shift_table(), deriv, precision=lax.Precision.HIGHEST).reshape(count, count, -1)
    signs = order_signs()[:, None]
    to_far = -jnp.einsum('kjp,jp->kp', spread, signs * near_moments, precision=lax.Precision.HIGHEST)
    to_near = -signs * jnp.einsum('kjp,jp->kp', spread, far_moments, precision=lax.Precision.HIGHEST)
    return (to_near * lives[None, :], to_far * lives[None, :])

def leaf_tile(near, far, codes, lives):
    shifts = ((codes // 9 - 1).astype(jnp.float32), (codes // 3 % 3 - 1).astype(jnp.float32), (codes % 3 - 1).astype(jnp.float32))
    parts = []
    for axis in range(3):
        moved = far[axis] + shifts[axis][:, None]
        parts.append(moved[:, None, :] - near[axis][:, :, None])
    squared = parts[0] * parts[0] + parts[1] * parts[1] + parts[2] * parts[2] + softening
    inverse = 1.0 / jnp.sqrt(squared)
    weight = inverse * inverse * inverse
    by_far = weight * far[3][:, None, :]
    by_near = weight * near[3][:, :, None]
    pull_near = jnp.stack([lax.optimization_barrier(jnp.sum(by_far * part, axis=2)) for part in parts])
    pull_far = jnp.stack([-lax.optimization_barrier(jnp.sum(by_near * part, axis=1)) for part in parts])
    return (pull_near * lives[None, :, None], pull_far * lives[None, :, None])

def pair_lists(links, local, per_domain, capacity):
    domain = jnp.arange(DOMAINS, dtype=jnp.int32)
    width = links.shape[3]
    slab = jnp.arange(SLABS, dtype=jnp.int32)[:, None]
    column = jnp.arange(width, dtype=jnp.int32)[None, :]
    peer = slab * SUBS + column // capacity
    owned = links[:, 0]
    first = domain[:, None, None] * per_domain + jnp.maximum(owned, 0)
    second = peer[None] * per_domain + links[:, 1]
    alive = (owned >= 0).astype(jnp.float32)
    firsts = jnp.concatenate([first.reshape(-1), (domain[:, None] * per_domain + local[:, 0]).reshape(-1)])
    seconds = jnp.concatenate([second.reshape(-1), (domain[:, None] * per_domain + local[:, 1]).reshape(-1)])
    codes = jnp.concatenate([links[:, 2].reshape(-1), local[:, 2].reshape(-1)])
    lives = jnp.concatenate([alive.reshape(-1), jnp.ones((local.shape[0] * local.shape[2],), jnp.float32)])
    return (firsts, seconds, codes, lives)

def sweep(tile, values, lists, width, initial):
    firsts, seconds, codes, lives = lists
    passes = firsts.shape[0] // width

    def step(held, item):
        first, second, code, live = item
        to_near, to_far = tile(values[:, first], values[:, second], code, live)
        return (held.at[:, first].add(to_near).at[:, second].add(to_far), None)
    items = tuple((entry.reshape(passes, width) for entry in (firsts, seconds, codes, lives)))
    held, _ = lax.scan(step, initial, items)
    return held

def reference(moments, positions, masses, counts, node_links, leaf_links, node_local, leaf_local):
    slot_index = jnp.arange(CELLS, dtype=jnp.int32)
    live_cells = (slot_index[None, :] < counts[:, None]).astype(jnp.float32)
    sources = jnp.concatenate([positions, (masses * live_cells)[None]], axis=0)
    node_lists = pair_lists(node_links, node_local, NODE_DEV, NCAP)
    node_total = node_lists[0].shape[0]
    local_exp = sweep(node_tile, moments, node_lists, math.gcd(node_total, 1024), jnp.zeros((COEFS, NODES), jnp.float32))
    leaf_lists = pair_lists(leaf_links, leaf_local, LEAF_DEV, LCAP)
    leaf_total = leaf_lists[0].shape[0]
    pull = sweep(leaf_tile, sources, leaf_lists, math.gcd(leaf_total, 64), jnp.zeros((3, LEAVES, CELLS), jnp.float32))
    return (local_exp, pull * live_cells[None])
```

```python
import functools

import jax
import jax.numpy as jnp
from jax import lax
from jax.experimental import pallas as pl
from jax.experimental.pallas import tpu as pltpu
from jax.sharding import PartitionSpec as P

softening = 0.04
DOMAINS = 256
SUBS = 32
SHIFTS = (32, -32, -2, -1, 2, 1)
F32, BF16, I32 = jnp.float32, jnp.bfloat16, jnp.int32
PEER_NODE, NODE_CODE, PEER_LEAF, LEAF_CODE, OWN_NODE = 25, 26, 27, 28, 29


def multi_indices():
    listed = []
    for order in range(5):
        for first in range(order, -1, -1):
            for second in range(order - first, -1, -1):
                listed.append((first, second, order - first - second))
    return listed


ALL = multi_indices()
KEPT = [entry for entry in ALL if entry[2] <= 1]
RANK = len(KEPT)


def reduce_rows(moments):
    rows = {entry: moments[number : number + 1, :] for number, entry in enumerate(ALL)}
    for entry in sorted(ALL, key=lambda item: -item[2]):
        first, second, third = entry
        if third > 1:
            for other in ((first + 2, second, third - 2), (first, second + 2, third - 2)):
                rows[other] = rows[other] - rows[entry]
    blank = jnp.zeros((32 - RANK, moments.shape[1]), F32)
    return jnp.concatenate([rows[entry] for entry in KEPT] + [blank], axis=0)


def expand_rows(total, out_ref):
    rows = {entry: total[number : number + 1, :] for number, entry in enumerate(KEPT)}
    for entry in sorted(ALL, key=lambda item: item[2]):
        first, second, third = entry
        if third > 1:
            rows[entry] = -(rows[first + 2, second, third - 2] + rows[first, second + 2, third - 2])
    for number, entry in enumerate(ALL):
        out_ref[number : number + 1, :] = rows[entry]


def split(value, terms):
    pieces = []
    for _ in range(terms - 1):
        high = value.astype(BF16)
        pieces.append(high)
        value = value - high.astype(F32)
    pieces.append(value.astype(BF16))
    return pieces


def one_hot(row, count):
    numbers = lax.broadcasted_iota(I32, (count, row.shape[1]), 0)
    return jnp.where(numbers == row, 1.0, 0.0).astype(BF16)


def pick(table3, hot):
    got = jnp.dot(table3, hot, preferred_element_type=F32)
    return got[0:32] + got[32:64] + got[64:96]


def put(values, hot):
    got = lax.dot_general(
        jnp.concatenate(split(values, 2), axis=0),
        hot,
        (((1,), (1,)), ((), ())),
        preferred_element_type=F32,
    )
    return got[0:32] + got[32:64]


def derivative_terms(codes):
    sep_x = ((codes * 1338) >> 16).astype(I32)
    rest = codes - sep_x * 49
    sep_y = (rest * 37) >> 8
    sep_z = rest - sep_y * 7
    sep = [(part - 3).astype(F32) for part in (sep_x, sep_y, sep_z)]
    squared = sep[0] * sep[0] + sep[1] * sep[1] + sep[2] * sep[2]
    inverse = lax.rsqrt(squared)
    inverse = inverse * (1.5 - 0.5 * squared * (inverse * inverse))
    inverse_sq = inverse * inverse
    known = {}
    power, factor = inverse, 1.0
    for level in range(5):
        known[0, 0, 0, level] = factor * power
        power = power * inverse_sq
        factor = factor * -(2 * level + 1)

    def term(first, second, third, level):
        key = (first, second, third, level)
        if key not in known:
            entry = [first, second, third]
            axis = 0 if first else (1 if second else 2)
            entry[axis] -= 1
            value = sep[axis] * term(*entry, level + 1)
            if entry[axis] > 0:
                scale = entry[axis]
                entry[axis] -= 1
                lower = term(*entry, level + 1)
                value = value + (lower if scale == 1 else scale * lower)
            known[key] = value
        return known[key]

    return {entry: term(*entry, 0) for entry in ALL if entry[2] <= 2}


def node_sums(codes, load_near, load_far, store_near, store_far):
    deriv = derivative_terms(codes)
    near = [load_near(number) for number in range(RANK)]
    far = [load_far(number) for number in range(RANK)]
    for k, left in enumerate(KEPT):
        even = {True: None, False: None}
        to_near = None
        for j, right in enumerate(KEPT):
            if sum(left) + sum(right) > 4:
                continue
            d = deriv[left[0] + right[0], left[1] + right[1], left[2] + right[2]]
            side = sum(right) % 2 == 0
            product = d * near[j]
            even[side] = product if even[side] is None else even[side] + product
            product = d * far[j]
            to_near = product if to_near is None else to_near + product
        to_far = -even[True] if even[False] is None else even[False] - even[True]
        store_far(k, to_far)
        store_near(k, to_near if sum(left) % 2 else -to_near)


def strided(ref, base, number):
    return ref[pl.ds(base + number, 8, stride=32), :]


def peer_of(shift):
    me = lax.axis_index("dx") * SUBS + lax.axis_index("dy")
    return (me + shift + DOMAINS) % DOMAINS


def pack_kernel(moments_hbm, nodes_hbm, leaves_hbm, kept_ref, sent_ref, moments_ref, nodes_ref, leaves_ref, sems):
    copies = [
        pltpu.make_async_copy(source, target, sems.at[number])
        for number, (source, target) in enumerate(
            ((nodes_hbm, nodes_ref), (leaves_hbm, leaves_ref), (moments_hbm, moments_ref))
        )
    ]
    for copy in copies:
        copy.start()
    for copy in copies:
        copy.wait()
    kept = reduce_rows(moments_ref[...])
    kept_ref[...] = kept
    table3 = jnp.concatenate(split(kept, 3), axis=0)
    own, peer_node, node_code = (nodes_ref[0, field] for field in range(3))
    leaf, peer_leaf, leaf_code = (leaves_ref[0, field] for field in range(3))
    fields = [
        own,
        jnp.where(own >= 0, peer_node, 0),
        jnp.where(own >= 0, node_code, 0),
        jnp.where(leaf >= 0, peer_leaf, -1),
        jnp.where(leaf >= 0, leaf_code, 0),
    ]
    stacked = jnp.concatenate([field.astype(F32) for field in fields], axis=0)
    source = lax.broadcasted_iota(I32, (128, 128), 0)
    target = lax.broadcasted_iota(I32, (128, 128), 1)
    lanes = jnp.where((source & 3) * 32 + (source >> 2) == target, 1.0, 0.0).astype(BF16)
    got = jnp.dot(jnp.concatenate(split(stacked, 2), axis=0), lanes, preferred_element_type=F32)
    moved = got[0:40] + got[40:80]
    block = lax.broadcasted_iota(I32, (128, 128), 0) >> 5 == (
        lax.broadcasted_iota(I32, (128, 128), 1) >> 5
    )
    row_number = lax.broadcasted_iota(I32, (8, 128), 0)
    for slab in range(8):
        rows = [moved[8 * field + slab : 8 * field + slab + 1] for field in range(5)]
        values = pick(table3, one_hot(rows[0].astype(I32), 256))
        last = values[24:32]
        for field, lane in ((0, OWN_NODE), (1, PEER_NODE), (2, NODE_CODE), (3, PEER_LEAF), (4, LEAF_CODE)):
            last = jnp.where(row_number == lane - 24, rows[field], last)
        values = jnp.concatenate([values[0:24], last], axis=0)
        turned = jnp.where(block, jnp.concatenate([values] * 4, axis=0), 0.0).T
        sent_ref[32 * slab : 32 * slab + 32, :] = (
            turned[0:32] + turned[32:64] + turned[64:96] + turned[96:128]
        )


def answer_kernel(
    links_ref, counts_ref, got_ref, kept_ref, positions_ref, masses_ref,
    reply_ref, partial_ref, asked_ref, cells_ref,
    turned, far_side, near_out, far_out, whole, rows, sems,
):
    whole[...] = got_ref[...].astype(I32)
    copies = []
    peers = [peer_of(shift) for shift in SHIFTS] + [peer_of(-shift) for shift in SHIFTS]
    for number in range(12):
        first = pl.multiple_of((peers[number] >> 3) * 8, 8)
        copies.append(
            pltpu.make_async_copy(whole.at[pl.ds(first, 8)], rows.at[number], sems.at[number])
        )
        copies[-1].start()
    for half in range(2):
        turned[128 * half : 128 * half + 128, :] = got_ref[128 * half : 128 * half + 128, :].T
    table3 = jnp.concatenate(split(kept_ref[...], 3), axis=0)
    for group in range(8):
        row = turned[32 * group + PEER_NODE : 32 * group + PEER_NODE + 1, :].astype(I32)
        far_side[32 * group : 32 * group + 32, :] = pick(table3, one_hot(row, 256))

    def store_near(number, value):
        near_out[pl.ds(number, 8, stride=32), :] = value

    def store_far(number, value):
        far_out[pl.ds(number, 8, stride=32), :] = value

    for number in range(RANK, 32):
        store_near(number, jnp.zeros((8, 128), F32))
        store_far(number, jnp.zeros((8, 128), F32))
    node_sums(
        strided(turned, 0, NODE_CODE).astype(I32),
        functools.partial(strided, turned, 0),
        functools.partial(strided, far_side, 0),
        store_near,
        store_far,
    )
    for half in range(2):
        reply_ref[128 * half : 128 * half + 128, :] = near_out[128 * half : 128 * half + 128, :].T
    total = jnp.zeros((32, 256), F32)
    for group in range(8):
        row = turned[32 * group + PEER_NODE : 32 * group + PEER_NODE + 1, :].astype(I32)
        total = total + put(far_out[32 * group : 32 * group + 32, :], one_hot(row, 256))
    partial_ref[...] = total
    for copy in copies:
        copy.wait()
    lane = lax.broadcasted_iota(I32, (1, 128), 1)

    def fill(number, slot, leaf):
        live = jnp.where(leaf >= 0, counts_ref[jnp.maximum(leaf, 0)], 0)
        leaf = jnp.maximum(leaf, 0)
        for axis in range(3):
            cells_ref[number, 4 * slot + axis : 4 * slot + axis + 1, :] = positions_ref[axis, pl.ds(leaf, 1), :]
        cells_ref[number, 4 * slot + 3 : 4 * slot + 4, :] = jnp.where(
            lane < live, masses_ref[pl.ds(leaf, 1), :], 0.0
        )

    for number in range(12):
        peer = peers[number]
        for slot in range(4):
            asked = rows[number, peer & 7, 32 * slot + PEER_LEAF]
            if number < 6:
                fill(number, slot, links_ref[0, 0, peer >> 5, (peer & 31) * 4 + slot])
                fill(number, 4 + slot, asked)
            else:
                asked_ref[number - 6, 2 * slot] = asked
                asked_ref[number - 6, 2 * slot + 1] = rows[number, peer & 7, 32 * slot + LEAF_CODE]


def leaf_offset(code):
    first = (code * 57) >> 9
    second = (code * 171) >> 9
    third = code - second * 3
    second = second - first * 3
    return [(part - 1).astype(F32) for part in (first, second, third)]


def eight_pairs(fields, left, right, terms_a, terms_b, sums_a, sums_b, pulls_a, pulls_b):
    a, b = ([fields[8 * (base + axis) : 8 * (base + axis) + 8, :] for axis in range(3)] for base in (0, 4))
    mass_a, mass_b = fields[24:32, :], fields[56:64, :]
    one = jnp.ones((8, 128), F32)
    rows_a, rows_b = [], []
    for axis in range(3):
        a1, a2, a3 = [part.astype(F32) for part in split(a[axis], 3)]
        b1, b2, b3 = [part.astype(F32) for part in split(-2.0 * b[axis], 3)]
        rows_a += [a1, a1, a2, a2, a1, a3]
        rows_b += [b1, b2, b1, b2, b3, b1]
    rows_a += [part.astype(F32) for part in split(a[0] * a[0] + a[1] * a[1] + a[2] * a[2] + softening, 3)]
    rows_b += [one] * 3
    rows_a += [one] * 3
    rows_b += [part.astype(F32) for part in split(b[0] * b[0] + b[1] * b[1] + b[2] * b[2], 3)]
    for number in range(24):
        left[pl.ds(number, 8, stride=32), :] = rows_a[number]
        right[pl.ds(number, 8, stride=32), :] = rows_b[number]
    sides = [(a, mass_a, terms_a)] + ([(b, mass_b, terms_b)] if terms_b is not None else [])
    for place, mass, terms in sides:
        for number, value in enumerate([mass * place[0], mass * place[1], mass * place[2], mass]):
            high, low = split(value, 2)
            terms[pl.ds(number, 8, stride=8), :] = high.astype(F32)
            terms[pl.ds(number + 4, 8, stride=8), :] = low.astype(F32)
    blank = jnp.zeros((32, 128), BF16)
    for group in range(2):
        turned = left[128 * group : 128 * group + 128, :].T.astype(BF16)
        block = right[128 * group : 128 * group + 128, :].astype(BF16)
        for half in range(2):
            columns = []
            for pair in (2 * half, 2 * half + 1):
                parts = [blank] * 4
                parts[pair] = block[32 * pair : 32 * pair + 32, :]
                columns.append(jnp.concatenate(parts, axis=0))
            squared = jnp.dot(turned, jnp.concatenate(columns, axis=1), preferred_element_type=F32)
            inverse = lax.rsqrt(squared)
            weight = inverse * (inverse * inverse)
            high, low = split(weight, 2)
            base = 8 * (4 * group + 2 * half)
            use = terms_a[base : base + 16, :].astype(BF16)
            got = jnp.dot(
                jnp.concatenate([use, use], axis=1),
                jnp.concatenate([high, low], axis=0),
                preferred_element_type=F32,
            )
            sums_b[base : base + 8, :] = got[0:8, 0:128]
            sums_b[base + 8 : base + 16, :] = got[8:16, 128:256]
            if terms_b is not None:
                use = terms_b[base : base + 16, :].astype(BF16)
                both = jnp.concatenate(
                    [
                        jnp.concatenate([high[:, 0:128], low[:, 0:128]], axis=1),
                        jnp.concatenate([high[:, 128:256], low[:, 128:256]], axis=1),
                    ],
                    axis=0,
                )
                got = lax.dot_general(
                    jnp.concatenate([use, use], axis=1),
                    both,
                    (((1,), (1,)), ((), ())),
                    preferred_element_type=F32,
                )
                sums_a[base : base + 8, :] = got[0:8, 0:128]
                sums_a[base + 8 : base + 16, :] = got[8:16, 128:256]
    results = [(b, sums_b, pulls_b)] + ([(a, sums_a, pulls_a)] if terms_b is not None else [])
    for own, sums, pulls in results:
        moved = [
            sums[pl.ds(number, 8, stride=8), :] + sums[pl.ds(number + 4, 8, stride=8), :] for number in range(4)
        ]
        for axis in range(3):
            pulls[8 * axis : 8 * axis + 8, :] = moved[axis] - own[axis] * moved[3]


def clear_rows(*refs):
    for ref in refs:
        for number in range(24, 32):
            ref[pl.ds(number, 8, stride=32), :] = jnp.zeros((8, 128), F32)


def local_nodes_kernel(pairs_ref, kept_ref, partial_ref, near_side, far_side, near_out, far_out):
    table3 = jnp.concatenate(split(kept_ref[...], 3), axis=0)
    for number in range(RANK, 32):
        near_out[pl.ds(number, 8, stride=32), :] = jnp.zeros((8, 128), F32)
        far_out[pl.ds(number, 8, stride=32), :] = jnp.zeros((8, 128), F32)
    total = jnp.zeros((32, 256), F32)
    for batch in range(2):
        code_rows = []
        for group in range(8):
            lanes = slice(1024 * batch + 128 * group, 1024 * batch + 128 * group + 128)
            first, second = (one_hot(pairs_ref[0, field : field + 1, lanes], 256) for field in range(2))
            near_side[32 * group : 32 * group + 32, :] = pick(table3, first)
            far_side[32 * group : 32 * group + 32, :] = pick(table3, second)
            code_rows.append(pairs_ref[0, 2:3, lanes])

        def store_near(number, value):
            near_out[pl.ds(number, 8, stride=32), :] = value

        def store_far(number, value):
            far_out[pl.ds(number, 8, stride=32), :] = value

        node_sums(
            jnp.concatenate(code_rows, axis=0),
            functools.partial(strided, near_side, 0),
            functools.partial(strided, far_side, 0),
            store_near,
            store_far,
        )
        for group in range(8):
            lanes = slice(1024 * batch + 128 * group, 1024 * batch + 128 * group + 128)
            first, second = (one_hot(pairs_ref[0, field : field + 1, lanes], 256) for field in range(2))
            total = total + put(near_out[32 * group : 32 * group + 32, :], first)
            total = total + put(far_out[32 * group : 32 * group + 32, :], second)
    partial_ref[...] = total


CHAINS = 4


def local_leaves_kernel(counts_ref, leaf_pairs_ref, positions_ref, masses_ref, pull_ref, *scratch):
    pull_ref[...] = jnp.zeros_like(pull_ref)
    sets = [scratch[9 * chain : 9 * chain + 9] for chain in range(CHAINS)]
    for work in sets:
        clear_rows(work[1], work[2])
    lane = lax.broadcasted_iota(I32, (1, 128), 1)

    def step(number, _):
        ends = []
        for chain, work in enumerate(sets):
            fields = work[0]
            for pair in range(8):
                place = (number * CHAINS + chain) * 8 + pair
                leaf = [leaf_pairs_ref[0, field, place] for field in range(2)]
                offset = leaf_offset(leaf_pairs_ref[0, 2, place])
                live = [counts_ref[leaf[side]] for side in range(2)]
                ends.append((leaf, live))
                for side, sign in ((0, -0.5), (1, 0.5)):
                    for axis in range(3):
                        row = 8 * (4 * side + axis) + pair
                        fields[row : row + 1, :] = positions_ref[axis, pl.ds(leaf[side], 1), :] + sign * offset[axis]
                    row = 8 * (4 * side + 3) + pair
                    fields[row : row + 1, :] = jnp.where(lane < live[side], masses_ref[pl.ds(leaf[side], 1), :], 0.0)
        for work in sets:
            eight_pairs(*work)
        for chain, work in enumerate(sets):
            for pair in range(8):
                leaf, live = ends[8 * chain + pair]
                for side, pulls in ((0, work[7]), (1, work[8])):
                    for axis in range(3):
                        pull_ref[axis, pl.ds(leaf[side], 1), :] += jnp.where(
                            lane < live[side], pulls[8 * axis + pair : 8 * axis + pair + 1, :], 0.0
                        )
        return 0

    lax.fori_loop(0, 16 // CHAINS, step, 0)


def final_kernel(
    links_ref, asked_ref, counts_ref, sent_ref, reply_ref, cross_ref, local_ref,
    cells0, cells1, cells2, cells3, cells4, cells5, positions_ref, pull_ref,
    out_ref, forces_ref,
    turned, turned_reply, fields, left, right, terms_a, sums_b, pulls_b,
):
    for half in range(2):
        part = slice(128 * half, 128 * half + 128)
        turned[part, :] = sent_ref[part, :].T
        turned_reply[part, :] = reply_ref[part, :].T
    total = cross_ref[...] + local_ref[...]
    for group in range(8):
        row = turned[32 * group + OWN_NODE : 32 * group + OWN_NODE + 1, :].astype(I32)
        total = total + put(turned_reply[32 * group : 32 * group + 32, :], one_hot(row, 256))
    expand_rows(total, out_ref)
    forces_ref[...] = pull_ref[...]
    clear_rows(left, right)
    lane = lax.broadcasted_iota(I32, (1, 128), 1)
    for number, cells in enumerate((cells0, cells1, cells2, cells3, cells4, cells5)):
        peer = peer_of(-SHIFTS[number])
        owns, lives = [], []
        for pair in range(8):
            slot = pair % 4
            if pair < 4:
                place = (peer >> 5, (peer & 31) * 4 + slot)
                own, code = links_ref[0, 0, place[0], place[1]], links_ref[0, 2, place[0], place[1]]
                source, sign = 4 + slot, 0.5
            else:
                own, code = asked_ref[number, 2 * slot], asked_ref[number, 2 * slot + 1]
                source, sign = slot, -0.5
            alive = own >= 0
            own = jnp.maximum(own, 0)
            offset = leaf_offset(jnp.where(alive, code, 0))
            owns.append(own)
            lives.append(jnp.where(alive, counts_ref[own], 0))
            for axis in range(3):
                row = 8 * axis + pair
                fields[row : row + 1, :] = (
                    cells[4 * source + axis : 4 * source + axis + 1, :] + sign * offset[axis]
                )
                fields[32 + row : 33 + row, :] = positions_ref[axis, pl.ds(own, 1), :] - sign * offset[axis]
            fields[24 + pair : 25 + pair, :] = cells[4 * source + 3 : 4 * source + 4, :]
        eight_pairs(fields, left, right, terms_a, None, None, sums_b, None, pulls_b)
        for pair in range(8):
            live = lane < lives[pair]
            for axis in range(3):
                forces_ref[axis, pl.ds(owns[pair], 1), :] += jnp.where(
                    live, pulls_b[8 * axis + pair : 8 * axis + pair + 1, :], 0.0
                )


SMEM = pl.BlockSpec(memory_space=pltpu.SMEM)
VMEM = pl.BlockSpec(memory_space=pltpu.VMEM)
HBM = pl.BlockSpec(memory_space=pltpu.HBM)
PARAMS = pltpu.CompilerParams(vmem_limit_bytes=32 * 1024 * 1024)


def exchange(sent):
    return lax.all_to_all(
        sent.reshape(DOMAINS, 1, 128), ("dx", "dy"), split_axis=0, concat_axis=0, tiled=True
    ).reshape(DOMAINS, 128)


def on_device(moments, positions, masses, counts, node_links, leaf_links, node_local, leaf_local):
    shape = jax.ShapeDtypeStruct
    block = pltpu.VMEM((256, 128), F32)
    tiles, pulls = pltpu.VMEM((64, 128), F32), pltpu.VMEM((24, 128), F32)
    kept, sent = pl.pallas_call(
        pack_kernel,
        out_shape=(shape((32, 256), F32), shape((256, 128), F32)),
        in_specs=[HBM] * 3,
        out_specs=(VMEM, VMEM),
        scratch_shapes=[
            pltpu.VMEM(moments.shape, F32),
            pltpu.VMEM(node_links.shape, I32),
            pltpu.VMEM(leaf_links.shape, I32),
            pltpu.SemaphoreType.DMA((3,)),
        ],
        compiler_params=PARAMS,
        name="pack",
    )(moments, node_links, leaf_links)
    got = exchange(sent)
    local_exp = pl.pallas_call(
        local_nodes_kernel,
        out_shape=shape((32, 256), F32),
        in_specs=[VMEM] * 2,
        out_specs=VMEM,
        scratch_shapes=[block] * 4,
        compiler_params=PARAMS,
        cost_estimate=pl.CostEstimate(flops=300_000_000, bytes_accessed=300_000, transcendentals=2048),
        name="local_nodes",
    )(node_local, kept)
    pull = pl.pallas_call(
        local_leaves_kernel,
        out_shape=shape(positions.shape, F32),
        in_specs=[SMEM, SMEM, VMEM, VMEM],
        out_specs=VMEM,
        scratch_shapes=[tiles, block, block, tiles, tiles, tiles, tiles, pulls, pulls] * CHAINS,
        compiler_params=PARAMS,
        cost_estimate=pl.CostEstimate(flops=80_000_000, bytes_accessed=3_000_000, transcendentals=2_100_000),
        name="local_leaves",
    )(counts, leaf_local, positions, masses)
    got, local_exp, pull = lax.optimization_barrier((got, local_exp, pull))
    reply, cross, asked, cells = pl.pallas_call(
        answer_kernel,
        out_shape=(
            shape((256, 128), F32),
            shape((32, 256), F32),
            shape((6, 8), I32),
            shape((6, 32, 128), F32),
        ),
        in_specs=[SMEM, SMEM] + [VMEM] * 4,
        out_specs=(VMEM, VMEM, SMEM, VMEM),
        scratch_shapes=[block] * 4
        + [pltpu.VMEM((256, 128), I32), pltpu.SMEM((12, 8, 128), I32), pltpu.SemaphoreType.DMA((12,))],
        compiler_params=PARAMS,
        name="answer",
    )(leaf_links, counts, got, kept, positions, masses)
    back = exchange(reply)
    moved = [
        lax.ppermute(
            cells[number],
            ("dx", "dy"),
            [(device, (device + shift) % DOMAINS) for device in range(DOMAINS)],
        )
        for number, shift in enumerate(SHIFTS)
    ]
    return pl.pallas_call(
        final_kernel,
        out_shape=(shape(moments.shape, F32), shape(positions.shape, F32)),
        in_specs=[SMEM] * 3 + [VMEM] * 12,
        out_specs=(VMEM, VMEM),
        scratch_shapes=[block, block, tiles, block, block, tiles, tiles, pulls],
        compiler_params=PARAMS,
        name="final",
    )(leaf_links, asked, counts, sent, back, cross, local_exp, *moved, positions, pull)


def solution(mesh):
    in_specs = (
        P(None, ("dx", "dy")),
        P(None, ("dx", "dy"), None),
        P(("dx", "dy"), None),
        P(("dx", "dy")),
        P(("dx", "dy"), None, None, None),
        P(("dx", "dy"), None, None, None),
        P(("dx", "dy"), None, None),
        P(("dx", "dy"), None, None),
    )
    out_specs = (P(None, ("dx", "dy")), P(None, ("dx", "dy"), None))
    return jax.shard_map(
        on_device, mesh=mesh, in_specs=in_specs, out_specs=out_specs, check_vma=False
    )
```

```python
import functools

import jax
import jax.numpy as jnp
from jax import lax
from jax.experimental import pallas as pl
from jax.experimental.pallas import tpu as pltpu
from jax.sharding import PartitionSpec as P

softening = 0.04
DOMAINS = 256
SUBS = 32
SHIFTS = (32, -32, -2, -1, 2, 1)
F32, BF16, I32 = jnp.float32, jnp.bfloat16, jnp.int32
PEER_NODE, NODE_CODE, PEER_LEAF, LEAF_CODE, OWN_NODE = 25, 26, 27, 28, 29


def multi_indices():
    listed = []
    for order in range(5):
        for first in range(order, -1, -1):
            for second in range(order - first, -1, -1):
                listed.append((first, second, order - first - second))
    return listed


ALL = multi_indices()
KEPT = [entry for entry in ALL if entry[2] <= 1]
RANK = len(KEPT)


def reduce_rows(moments):
    rows = {entry: moments[number : number + 1, :] for number, entry in enumerate(ALL)}
    for entry in sorted(ALL, key=lambda item: -item[2]):
        first, second, third = entry
        if third > 1:
            for other in ((first + 2, second, third - 2), (first, second + 2, third - 2)):
                rows[other] = rows[other] - rows[entry]
    blank = jnp.zeros((32 - RANK, moments.shape[1]), F32)
    return jnp.concatenate([rows[entry] for entry in KEPT] + [blank], axis=0)


def expand_rows(total, out_ref):
    rows = {entry: total[number : number + 1, :] for number, entry in enumerate(KEPT)}
    for entry in sorted(ALL, key=lambda item: item[2]):
        first, second, third = entry
        if third > 1:
            rows[entry] = -(rows[first + 2, second, third - 2] + rows[first, second + 2, third - 2])
    for number, entry in enumerate(ALL):
        out_ref[number : number + 1, :] = rows[entry]


def split(value, terms):
    pieces = []
    for _ in range(terms - 1):
        high = value.astype(BF16)
        pieces.append(high)
        value = value - high.astype(F32)
    pieces.append(value.astype(BF16))
    return pieces


def one_hot(row, count):
    numbers = lax.broadcasted_iota(I32, (count, row.shape[1]), 0)
    return jnp.where(numbers == row, 1.0, 0.0).astype(BF16)


def pick(table3, hot):
    got = jnp.dot(table3, hot, preferred_element_type=F32)
    return got[0:32] + got[32:64] + got[64:96]


def put(values, hot):
    got = lax.dot_general(
        jnp.concatenate(split(values, 2), axis=0),
        hot,
        (((1,), (1,)), ((), ())),
        preferred_element_type=F32,
    )
    return got[0:32] + got[32:64]


def derivative_terms(codes):
    sep_x = ((codes * 1338) >> 16).astype(I32)
    rest = codes - sep_x * 49
    sep_y = (rest * 37) >> 8
    sep_z = rest - sep_y * 7
    sep = [(part - 3).astype(F32) for part in (sep_x, sep_y, sep_z)]
    squared = sep[0] * sep[0] + sep[1] * sep[1] + sep[2] * sep[2]
    inverse = lax.rsqrt(squared)
    inverse = inverse * (1.5 - 0.5 * squared * (inverse * inverse))
    inverse_sq = inverse * inverse
    known = {}
    power, factor = inverse, 1.0
    for level in range(5):
        known[0, 0, 0, level] = factor * power
        power = power * inverse_sq
        factor = factor * -(2 * level + 1)

    def term(first, second, third, level):
        key = (first, second, third, level)
        if key not in known:
            entry = [first, second, third]
            axis = 0 if first else (1 if second else 2)
            entry[axis] -= 1
            value = sep[axis] * term(*entry, level + 1)
            if entry[axis] > 0:
                scale = entry[axis]
                entry[axis] -= 1
                lower = term(*entry, level + 1)
                value = value + (lower if scale == 1 else scale * lower)
            known[key] = value
        return known[key]

    return {entry: term(*entry, 0) for entry in ALL if entry[2] <= 2}


def node_sums(codes, load_near, load_far, store_near, store_far):
    deriv = derivative_terms(codes)
    near = [load_near(number) for number in range(RANK)]
    far = [load_far(number) for number in range(RANK)]
    for k, left in enumerate(KEPT):
        even = {True: None, False: None}
        to_near = None
        for j, right in enumerate(KEPT):
            if sum(left) + sum(right) > 4:
                continue
            d = deriv[left[0] + right[0], left[1] + right[1], left[2] + right[2]]
            side = sum(right) % 2 == 0
            product = d * near[j]
            even[side] = product if even[side] is None else even[side] + product
            product = d * far[j]
            to_near = product if to_near is None else to_near + product
        to_far = -even[True] if even[False] is None else even[False] - even[True]
        store_far(k, to_far)
        store_near(k, to_near if sum(left) % 2 else -to_near)


def strided(ref, base, number):
    return ref[pl.ds(base + number, 8, stride=32), :]


def peer_of(shift):
    me = lax.axis_index("dx") * SUBS + lax.axis_index("dy")
    return (me + shift + DOMAINS) % DOMAINS


def pack_kernel(moments_hbm, nodes_hbm, leaves_hbm, kept_ref, sent_ref, moments_ref, nodes_ref, leaves_ref, sems):
    copies = [
        pltpu.make_async_copy(source, target, sems.at[number])
        for number, (source, target) in enumerate(
            ((nodes_hbm, nodes_ref), (leaves_hbm, leaves_ref), (moments_hbm, moments_ref))
        )
    ]
    for copy in copies:
        copy.start()
    for copy in copies:
        copy.wait()
    kept = reduce_rows(moments_ref[...])
    kept_ref[...] = kept
    table3 = jnp.concatenate(split(kept, 3), axis=0)
    own, peer_node, node_code = (nodes_ref[0, field] for field in range(3))
    leaf, peer_leaf, leaf_code = (leaves_ref[0, field] for field in range(3))
    fields = [
        own,
        jnp.where(own >= 0, peer_node, 0),
        jnp.where(own >= 0, node_code, 0),
        jnp.where(leaf >= 0, peer_leaf, -1),
        jnp.where(leaf >= 0, leaf_code, 0),
    ]
    stacked = jnp.concatenate([field.astype(F32) for field in fields], axis=0)
    source = lax.broadcasted_iota(I32, (128, 128), 0)
    target = lax.broadcasted_iota(I32, (128, 128), 1)
    lanes = jnp.where((source & 3) * 32 + (source >> 2) == target, 1.0, 0.0).astype(BF16)
    got = jnp.dot(jnp.concatenate(split(stacked, 2), axis=0), lanes, preferred_element_type=F32)
    moved = got[0:40] + got[40:80]
    block = lax.broadcasted_iota(I32, (128, 128), 0) >> 5 == (
        lax.broadcasted_iota(I32, (128, 128), 1) >> 5
    )
    row_number = lax.broadcasted_iota(I32, (8, 128), 0)
    for slab in range(8):
        rows = [moved[8 * field + slab : 8 * field + slab + 1] for field in range(5)]
        values = pick(table3, one_hot(rows[0].astype(I32), 256))
        last = values[24:32]
        for field, lane in ((0, OWN_NODE), (1, PEER_NODE), (2, NODE_CODE), (3, PEER_LEAF), (4, LEAF_CODE)):
            last = jnp.where(row_number == lane - 24, rows[field], last)
        values = jnp.concatenate([values[0:24], last], axis=0)
        turned = jnp.where(block, jnp.concatenate([values] * 4, axis=0), 0.0).T
        sent_ref[32 * slab : 32 * slab + 32, :] = (
            turned[0:32] + turned[32:64] + turned[64:96] + turned[96:128]
        )


def answer_kernel(
    links_ref, counts_ref, got_ref, kept_ref, positions_ref, masses_ref,
    reply_ref, partial_ref, asked_ref, cells_ref,
    turned, far_side, near_out, far_out, whole, rows, sems,
):
    whole[...] = got_ref[...].astype(I32)
    copies = []
    peers = [peer_of(shift) for shift in SHIFTS] + [peer_of(-shift) for shift in SHIFTS]
    for number in range(12):
        first = pl.multiple_of((peers[number] >> 3) * 8, 8)
        copies.append(
            pltpu.make_async_copy(whole.at[pl.ds(first, 8)], rows.at[number], sems.at[number])
        )
        copies[-1].start()
    for half in range(2):
        turned[128 * half : 128 * half + 128, :] = got_ref[128 * half : 128 * half + 128, :].T
    table3 = jnp.concatenate(split(kept_ref[...], 3), axis=0)
    for group in range(8):
        row = turned[32 * group + PEER_NODE : 32 * group + PEER_NODE + 1, :].astype(I32)
        far_side[32 * group : 32 * group + 32, :] = pick(table3, one_hot(row, 256))

    def store_near(number, value):
        near_out[pl.ds(number, 8, stride=32), :] = value

    def store_far(number, value):
        far_out[pl.ds(number, 8, stride=32), :] = value

    for number in range(RANK, 32):
        store_near(number, jnp.zeros((8, 128), F32))
        store_far(number, jnp.zeros((8, 128), F32))
    node_sums(
        strided(turned, 0, NODE_CODE).astype(I32),
        functools.partial(strided, turned, 0),
        functools.partial(strided, far_side, 0),
        store_near,
        store_far,
    )
    for half in range(2):
        reply_ref[128 * half : 128 * half + 128, :] = near_out[128 * half : 128 * half + 128, :].T
    total = jnp.zeros((32, 256), F32)
    for group in range(8):
        row = turned[32 * group + PEER_NODE : 32 * group + PEER_NODE + 1, :].astype(I32)
        total = total + put(far_out[32 * group : 32 * group + 32, :], one_hot(row, 256))
    partial_ref[...] = total
    for copy in copies:
        copy.wait()
    lane = lax.broadcasted_iota(I32, (1, 128), 1)

    def fill(number, slot, leaf):
        live = jnp.where(leaf >= 0, counts_ref[jnp.maximum(leaf, 0)], 0)
        leaf = jnp.maximum(leaf, 0)
        for axis in range(3):
            cells_ref[number, 4 * slot + axis : 4 * slot + axis + 1, :] = positions_ref[axis, pl.ds(leaf, 1), :]
        cells_ref[number, 4 * slot + 3 : 4 * slot + 4, :] = jnp.where(
            lane < live, masses_ref[pl.ds(leaf, 1), :], 0.0
        )

    for number in range(12):
        peer = peers[number]
        for slot in range(4):
            asked = rows[number, peer & 7, 32 * slot + PEER_LEAF]
            if number < 6:
                fill(number, slot, links_ref[0, 0, peer >> 5, (peer & 31) * 4 + slot])
                fill(number, 4 + slot, asked)
            else:
                asked_ref[number - 6, 2 * slot] = asked
                asked_ref[number - 6, 2 * slot + 1] = rows[number, peer & 7, 32 * slot + LEAF_CODE]


def leaf_offset(code):
    first = (code * 57) >> 9
    second = (code * 171) >> 9
    third = code - second * 3
    second = second - first * 3
    return [(part - 1).astype(F32) for part in (first, second, third)]


def eight_pairs(fields, left, right, terms_a, terms_b, sums_a, sums_b, pulls_a, pulls_b):
    a, b = ([fields[8 * (base + axis) : 8 * (base + axis) + 8, :] for axis in range(3)] for base in (0, 4))
    mass_a, mass_b = fields[24:32, :], fields[56:64, :]
    one = jnp.ones((8, 128), F32)
    rows_a, rows_b = [], []
    for axis in range(3):
        a1, a2, a3 = [part.astype(F32) for part in split(a[axis], 3)]
        b1, b2, b3 = [part.astype(F32) for part in split(-2.0 * b[axis], 3)]
        rows_a += [a1, a1, a2, a2, a1, a3]
        rows_b += [b1, b2, b1, b2, b3, b1]
    rows_a += [part.astype(F32) for part in split(a[0] * a[0] + a[1] * a[1] + a[2] * a[2] + softening, 3)]
    rows_b += [one] * 3
    rows_a += [one] * 3
    rows_b += [part.astype(F32) for part in split(b[0] * b[0] + b[1] * b[1] + b[2] * b[2], 3)]
    for number in range(24):
        left[pl.ds(number, 8, stride=32), :] = rows_a[number]
        right[pl.ds(number, 8, stride=32), :] = rows_b[number]
    sides = [(a, mass_a, terms_a)] + ([(b, mass_b, terms_b)] if terms_b is not None else [])
    for place, mass, terms in sides:
        for number, value in enumerate([mass * place[0], mass * place[1], mass * place[2], mass]):
            high, low = split(value, 2)
            terms[pl.ds(number, 8, stride=8), :] = high.astype(F32)
            terms[pl.ds(number + 4, 8, stride=8), :] = low.astype(F32)
    blank = jnp.zeros((32, 128), BF16)
    for group in range(2):
        turned = left[128 * group : 128 * group + 128, :].T.astype(BF16)
        block = right[128 * group : 128 * group + 128, :].astype(BF16)
        for half in range(2):
            columns = []
            for pair in (2 * half, 2 * half + 1):
                parts = [blank] * 4
                parts[pair] = block[32 * pair : 32 * pair + 32, :]
                columns.append(jnp.concatenate(parts, axis=0))
            squared = jnp.dot(turned, jnp.concatenate(columns, axis=1), preferred_element_type=F32)
            inverse = lax.rsqrt(squared)
            weight = inverse * (inverse * inverse)
            high, low = split(weight, 2)
            base = 8 * (4 * group + 2 * half)
            use = terms_a[base : base + 16, :].astype(BF16)
            got = jnp.dot(
                jnp.concatenate([use, use], axis=1),
                jnp.concatenate([high, low], axis=0),
                preferred_element_type=F32,
            )
            sums_b[base : base + 8, :] = got[0:8, 0:128]
            sums_b[base + 8 : base + 16, :] = got[8:16, 128:256]
            if terms_b is not None:
                use = terms_b[base : base + 16, :].astype(BF16)
                both = jnp.concatenate(
                    [
                        jnp.concatenate([high[:, 0:128], low[:, 0:128]], axis=1),
                        jnp.concatenate([high[:, 128:256], low[:, 128:256]], axis=1),
                    ],
                    axis=0,
                )
                got = lax.dot_general(
                    jnp.concatenate([use, use], axis=1),
                    both,
                    (((1,), (1,)), ((), ())),
                    preferred_element_type=F32,
                )
                sums_a[base : base + 8, :] = got[0:8, 0:128]
                sums_a[base + 8 : base + 16, :] = got[8:16, 128:256]
    results = [(b, sums_b, pulls_b)] + ([(a, sums_a, pulls_a)] if terms_b is not None else [])
    for own, sums, pulls in results:
        moved = [
            sums[pl.ds(number, 8, stride=8), :] + sums[pl.ds(number + 4, 8, stride=8), :] for number in range(4)
        ]
        for axis in range(3):
            pulls[8 * axis : 8 * axis + 8, :] = moved[axis] - own[axis] * moved[3]


def clear_rows(*refs):
    for ref in refs:
        for number in range(24, 32):
            ref[pl.ds(number, 8, stride=32), :] = jnp.zeros((8, 128), F32)


def local_nodes_kernel(pairs_ref, kept_ref, partial_ref, near_side, far_side, near_out, far_out):
    table3 = jnp.concatenate(split(kept_ref[...], 3), axis=0)
    for number in range(RANK, 32):
        near_out[pl.ds(number, 8, stride=32), :] = jnp.zeros((8, 128), F32)
        far_out[pl.ds(number, 8, stride=32), :] = jnp.zeros((8, 128), F32)
    total = jnp.zeros((32, 256), F32)
    for batch in range(2):
        code_rows = []
        for group in range(8):
            lanes = slice(1024 * batch + 128 * group, 1024 * batch + 128 * group + 128)
            first, second = (one_hot(pairs_ref[0, field : field + 1, lanes], 256) for field in range(2))
            near_side[32 * group : 32 * group + 32, :] = pick(table3, first)
            far_side[32 * group : 32 * group + 32, :] = pick(table3, second)
            code_rows.append(pairs_ref[0, 2:3, lanes])

        def store_near(number, value):
            near_out[pl.ds(number, 8, stride=32), :] = value

        def store_far(number, value):
            far_out[pl.ds(number, 8, stride=32), :] = value

        node_sums(
            jnp.concatenate(code_rows, axis=0),
            functools.partial(strided, near_side, 0),
            functools.partial(strided, far_side, 0),
            store_near,
            store_far,
        )
        for group in range(8):
            lanes = slice(1024 * batch + 128 * group, 1024 * batch + 128 * group + 128)
            first, second = (one_hot(pairs_ref[0, field : field + 1, lanes], 256) for field in range(2))
            total = total + put(near_out[32 * group : 32 * group + 32, :], first)
            total = total + put(far_out[32 * group : 32 * group + 32, :], second)
    partial_ref[...] = total


CHAINS = 4
EARLY = 3


def gather_pairs(sets, first_place, counts_ref, leaf_pairs_ref, positions_ref, masses_ref):
    lane = lax.broadcasted_iota(I32, (1, 128), 1)
    for chain, work in enumerate(sets):
        fields = work[0]
        for pair in range(8):
            place = first_place + chain * 8 + pair
            leaf = [leaf_pairs_ref[0, field, place] for field in range(2)]
            offset = leaf_offset(leaf_pairs_ref[0, 2, place])
            for side, sign in ((0, -0.5), (1, 0.5)):
                live = counts_ref[leaf[side]]
                for axis in range(3):
                    row = 8 * (4 * side + axis) + pair
                    fields[row : row + 1, :] = positions_ref[axis, pl.ds(leaf[side], 1), :] + sign * offset[axis]
                row = 8 * (4 * side + 3) + pair
                fields[row : row + 1, :] = jnp.where(lane < live, masses_ref[pl.ds(leaf[side], 1), :], 0.0)


def scatter_pairs(pulls_of, first_place, counts_ref, leaf_pairs_ref, pull_ref):
    lane = lax.broadcasted_iota(I32, (1, 128), 1)
    for chain in range(CHAINS):
        for pair in range(8):
            place = first_place + chain * 8 + pair
            for side in range(2):
                leaf = leaf_pairs_ref[0, side, place]
                live = lane < counts_ref[leaf]
                for axis in range(3):
                    pull_ref[axis, pl.ds(leaf, 1), :] += jnp.where(
                        live, pulls_of(chain, side, 8 * axis + pair), 0.0
                    )


def local_leaves_kernel(counts_ref, leaf_pairs_ref, positions_ref, masses_ref, pull_ref, *scratch):
    pull_ref[...] = jnp.zeros_like(pull_ref)
    sets = [scratch[9 * chain : 9 * chain + 9] for chain in range(CHAINS)]
    for work in sets:
        clear_rows(work[1], work[2])

    def step(number, _):
        place = number * (8 * CHAINS)
        gather_pairs(sets, place, counts_ref, leaf_pairs_ref, positions_ref, masses_ref)
        for work in sets:
            eight_pairs(*work)
        scatter_pairs(
            lambda chain, side, row: sets[chain][7 + side][row : row + 1, :],
            place, counts_ref, leaf_pairs_ref, pull_ref,
        )
        return 0

    lax.fori_loop(0, EARLY, step, 0)


def late_leaves_kernel(counts_ref, leaf_pairs_ref, positions_ref, masses_ref, late_ref, *scratch):
    sets = [scratch[9 * chain : 9 * chain + 9] for chain in range(CHAINS)]
    for work in sets:
        clear_rows(work[1], work[2])
    gather_pairs(sets, EARLY * 8 * CHAINS, counts_ref, leaf_pairs_ref, positions_ref, masses_ref)
    for chain, work in enumerate(sets):
        eight_pairs(*work)
        for side in range(2):
            late_ref[chain, side] = work[7 + side][...]


def final_kernel(
    links_ref, asked_ref, counts_ref, sent_ref, reply_ref, cross_ref, local_ref,
    cells0, cells1, cells2, cells3, cells4, cells5, positions_ref, pull_ref, late_ref, leaf_pairs_ref,
    out_ref, forces_ref,
    turned, turned_reply, fields, left, right, terms_a, sums_b, pulls_b,
):
    for half in range(2):
        part = slice(128 * half, 128 * half + 128)
        turned[part, :] = sent_ref[part, :].T
        turned_reply[part, :] = reply_ref[part, :].T
    total = cross_ref[...] + local_ref[...]
    for group in range(8):
        row = turned[32 * group + OWN_NODE : 32 * group + OWN_NODE + 1, :].astype(I32)
        total = total + put(turned_reply[32 * group : 32 * group + 32, :], one_hot(row, 256))
    expand_rows(total, out_ref)
    forces_ref[...] = pull_ref[...]
    scatter_pairs(
        lambda chain, side, row: late_ref[chain, side, row : row + 1, :],
        EARLY * 8 * CHAINS, counts_ref, leaf_pairs_ref, forces_ref,
    )
    clear_rows(left, right)
    lane = lax.broadcasted_iota(I32, (1, 128), 1)
    for number, cells in enumerate((cells0, cells1, cells2, cells3, cells4, cells5)):
        peer = peer_of(-SHIFTS[number])
        owns, lives = [], []
        for pair in range(8):
            slot = pair % 4
            if pair < 4:
                place = (peer >> 5, (peer & 31) * 4 + slot)
                own, code = links_ref[0, 0, place[0], place[1]], links_ref[0, 2, place[0], place[1]]
                source, sign = 4 + slot, 0.5
            else:
                own, code = asked_ref[number, 2 * slot], asked_ref[number, 2 * slot + 1]
                source, sign = slot, -0.5
            alive = own >= 0
            own = jnp.maximum(own, 0)
            offset = leaf_offset(jnp.where(alive, code, 0))
            owns.append(own)
            lives.append(jnp.where(alive, counts_ref[own], 0))
            for axis in range(3):
                row = 8 * axis + pair
                fields[row : row + 1, :] = (
                    cells[4 * source + axis : 4 * source + axis + 1, :] + sign * offset[axis]
                )
                fields[32 + row : 33 + row, :] = positions_ref[axis, pl.ds(own, 1), :] - sign * offset[axis]
            fields[24 + pair : 25 + pair, :] = cells[4 * source + 3 : 4 * source + 4, :]
        eight_pairs(fields, left, right, terms_a, None, None, sums_b, None, pulls_b)
        for pair in range(8):
            live = lane < lives[pair]
            for axis in range(3):
                forces_ref[axis, pl.ds(owns[pair], 1), :] += jnp.where(
                    live, pulls_b[8 * axis + pair : 8 * axis + pair + 1, :], 0.0
                )


SMEM = pl.BlockSpec(memory_space=pltpu.SMEM)
VMEM = pl.BlockSpec(memory_space=pltpu.VMEM)
HBM = pl.BlockSpec(memory_space=pltpu.HBM)
PARAMS = pltpu.CompilerParams(vmem_limit_bytes=32 * 1024 * 1024)


def exchange(sent):
    return lax.all_to_all(
        sent.reshape(DOMAINS, 1, 128), ("dx", "dy"), split_axis=0, concat_axis=0, tiled=True
    ).reshape(DOMAINS, 128)


def on_device(moments, positions, masses, counts, node_links, leaf_links, node_local, leaf_local):
    shape = jax.ShapeDtypeStruct
    block = pltpu.VMEM((256, 128), F32)
    tiles, pulls = pltpu.VMEM((64, 128), F32), pltpu.VMEM((24, 128), F32)
    kept, sent = pl.pallas_call(
        pack_kernel,
        out_shape=(shape((32, 256), F32), shape((256, 128), F32)),
        in_specs=[HBM] * 3,
        out_specs=(VMEM, VMEM),
        scratch_shapes=[
            pltpu.VMEM(moments.shape, F32),
            pltpu.VMEM(node_links.shape, I32),
            pltpu.VMEM(leaf_links.shape, I32),
            pltpu.SemaphoreType.DMA((3,)),
        ],
        compiler_params=pltpu.CompilerParams(vmem_limit_bytes=56 * 1024 * 1024),
        name="pack",
    )(moments, node_links, leaf_links)
    got = exchange(sent)
    pull = pl.pallas_call(
        local_leaves_kernel,
        out_shape=shape(positions.shape, F32),
        in_specs=[SMEM, SMEM, VMEM, VMEM],
        out_specs=VMEM,
        scratch_shapes=[tiles, block, block, tiles, tiles, tiles, tiles, pulls, pulls] * CHAINS,
        compiler_params=PARAMS,
        cost_estimate=pl.CostEstimate(flops=80_000_000, bytes_accessed=3_000_000, transcendentals=2_100_000),
        name="local_leaves",
    )(counts, leaf_local, positions, masses)
    got, pull = lax.optimization_barrier((got, pull))
    reply, cross, asked, cells = pl.pallas_call(
        answer_kernel,
        out_shape=(
            shape((256, 128), F32),
            shape((32, 256), F32),
            shape((6, 8), I32),
            shape((6, 32, 128), F32),
        ),
        in_specs=[SMEM, SMEM] + [VMEM] * 4,
        out_specs=(VMEM, VMEM, SMEM, VMEM),
        scratch_shapes=[block] * 4
        + [pltpu.VMEM((256, 128), I32), pltpu.SMEM((12, 8, 128), I32), pltpu.SemaphoreType.DMA((12,))],
        compiler_params=PARAMS,
        name="answer",
    )(leaf_links, counts, got, kept, positions, masses)
    back = exchange(reply)
    moved = [
        lax.ppermute(
            cells[number],
            ("dx", "dy"),
            [(device, (device + shift) % DOMAINS) for device in range(DOMAINS)],
        )
        for number, shift in enumerate(SHIFTS)
    ]
    kept_late, leaf_pairs_late, moved[5] = lax.optimization_barrier((kept, leaf_local, moved[5]))
    local_exp = pl.pallas_call(
        local_nodes_kernel,
        out_shape=shape((32, 256), F32),
        in_specs=[VMEM] * 2,
        out_specs=VMEM,
        scratch_shapes=[block] * 4,
        compiler_params=PARAMS,
        cost_estimate=pl.CostEstimate(flops=300_000_000, bytes_accessed=300_000, transcendentals=2048),
        name="local_nodes",
    )(node_local, kept_late)
    late = pl.pallas_call(
        late_leaves_kernel,
        out_shape=shape((CHAINS, 2, 24, 128), F32),
        in_specs=[SMEM, SMEM, VMEM, VMEM],
        out_specs=VMEM,
        scratch_shapes=[tiles, block, block, tiles, tiles, tiles, tiles, pulls, pulls] * CHAINS,
        compiler_params=PARAMS,
        cost_estimate=pl.CostEstimate(flops=20_000_000, bytes_accessed=1_500_000, transcendentals=500_000),
        name="late_leaves",
    )(counts, leaf_pairs_late, positions, masses)
    return pl.pallas_call(
        final_kernel,
        out_shape=(shape(moments.shape, F32), shape(positions.shape, F32)),
        in_specs=[SMEM] * 3 + [VMEM] * 13 + [SMEM],
        out_specs=(VMEM, VMEM),
        scratch_shapes=[block, block, tiles, block, block, tiles, tiles, pulls],
        compiler_params=PARAMS,
        name="final",
    )(leaf_links, asked, counts, sent, back, cross, local_exp, *moved, positions, pull, late, leaf_local)


def solution(mesh):
    in_specs = (
        P(None, ("dx", "dy")),
        P(None, ("dx", "dy"), None),
        P(("dx", "dy"), None),
        P(("dx", "dy")),
        P(("dx", "dy"), None, None, None),
        P(("dx", "dy"), None, None, None),
        P(("dx", "dy"), None, None),
        P(("dx", "dy"), None, None),
    )
    out_specs = (P(None, ("dx", "dy")), P(None, ("dx", "dy"), None))
    return jax.shard_map(
        on_device, mesh=mesh, in_specs=in_specs, out_specs=out_specs, check_vma=False
    )
```

```python
import functools

import jax
import jax.numpy as jnp
from jax import lax
from jax.experimental import pallas as pl
from jax.experimental.pallas import tpu as pltpu
from jax.sharding import PartitionSpec as P

softening = 0.04
DOMAINS = 256
SUBS = 32
SHIFTS = (32, -32, -2, -1, 2, 1)
F32, BF16, I32 = jnp.float32, jnp.bfloat16, jnp.int32
PEER_NODE, NODE_CODE, PEER_LEAF, LEAF_CODE, OWN_NODE = 25, 26, 27, 28, 29


def multi_indices():
    listed = []
    for order in range(5):
        for first in range(order, -1, -1):
            for second in range(order - first, -1, -1):
                listed.append((first, second, order - first - second))
    return listed


ALL = multi_indices()
KEPT = [entry for entry in ALL if entry[2] <= 1]
RANK = len(KEPT)


def reduce_rows(moments):
    rows = {entry: moments[number : number + 1, :] for number, entry in enumerate(ALL)}
    for entry in sorted(ALL, key=lambda item: -item[2]):
        first, second, third = entry
        if third > 1:
            for other in ((first + 2, second, third - 2), (first, second + 2, third - 2)):
                rows[other] = rows[other] - rows[entry]
    blank = jnp.zeros((32 - RANK, moments.shape[1]), F32)
    return jnp.concatenate([rows[entry] for entry in KEPT] + [blank], axis=0)


def expand_rows(total, out_ref):
    rows = {entry: total[number : number + 1, :] for number, entry in enumerate(KEPT)}
    for entry in sorted(ALL, key=lambda item: item[2]):
        first, second, third = entry
        if third > 1:
            rows[entry] = -(rows[first + 2, second, third - 2] + rows[first, second + 2, third - 2])
    for number, entry in enumerate(ALL):
        out_ref[number : number + 1, :] = rows[entry]


def split(value, terms):
    pieces = []
    for _ in range(terms - 1):
        high = value.astype(BF16)
        pieces.append(high)
        value = value - high.astype(F32)
    pieces.append(value.astype(BF16))
    return pieces


def one_hot(row, count):
    numbers = lax.broadcasted_iota(I32, (count, row.shape[1]), 0)
    return jnp.where(numbers == row, 1.0, 0.0).astype(BF16)


def pick(table3, hot):
    got = jnp.dot(table3, hot, preferred_element_type=F32)
    return got[0:32] + got[32:64] + got[64:96]


def put(values, hot):
    got = lax.dot_general(
        jnp.concatenate(split(values, 2), axis=0),
        hot,
        (((1,), (1,)), ((), ())),
        preferred_element_type=F32,
    )
    return got[0:32] + got[32:64]


def derivative_terms(codes):
    sep_x = ((codes * 1338) >> 16).astype(I32)
    rest = codes - sep_x * 49
    sep_y = (rest * 37) >> 8
    sep_z = rest - sep_y * 7
    sep = [(part - 3).astype(F32) for part in (sep_x, sep_y, sep_z)]
    squared = sep[0] * sep[0] + sep[1] * sep[1] + sep[2] * sep[2]
    inverse = lax.rsqrt(squared)
    inverse = inverse * (1.5 - 0.5 * squared * (inverse * inverse))
    inverse_sq = inverse * inverse
    known = {}
    power, factor = inverse, 1.0
    for level in range(5):
        known[0, 0, 0, level] = factor * power
        power = power * inverse_sq
        factor = factor * -(2 * level + 1)

    def term(first, second, third, level):
        key = (first, second, third, level)
        if key not in known:
            entry = [first, second, third]
            axis = 0 if first else (1 if second else 2)
            entry[axis] -= 1
            value = sep[axis] * term(*entry, level + 1)
            if entry[axis] > 0:
                scale = entry[axis]
                entry[axis] -= 1
                lower = term(*entry, level + 1)
                value = value + (lower if scale == 1 else scale * lower)
            known[key] = value
        return known[key]

    return {entry: term(*entry, 0) for entry in ALL if entry[2] <= 2}


def node_sums(codes, load_near, load_far, store_near, store_far):
    deriv = derivative_terms(codes)
    near = [load_near(number) for number in range(RANK)]
    far = [load_far(number) for number in range(RANK)]
    for k, left in enumerate(KEPT):
        even = {True: None, False: None}
        to_near = None
        for j, right in enumerate(KEPT):
            if sum(left) + sum(right) > 4:
                continue
            d = deriv[left[0] + right[0], left[1] + right[1], left[2] + right[2]]
            side = sum(right) % 2 == 0
            product = d * near[j]
            even[side] = product if even[side] is None else even[side] + product
            product = d * far[j]
            to_near = product if to_near is None else to_near + product
        to_far = -even[True] if even[False] is None else even[False] - even[True]
        store_far(k, to_far)
        store_near(k, to_near if sum(left) % 2 else -to_near)


def strided(ref, base, number):
    return ref[pl.ds(base + number, 8, stride=32), :]


def peer_of(shift):
    me = lax.axis_index("dx") * SUBS + lax.axis_index("dy")
    return (me + shift + DOMAINS) % DOMAINS


def pack_kernel(moments_hbm, nodes_hbm, leaves_hbm, kept_ref, sent_ref, moments_ref, nodes_ref, leaves_ref, sems):
    copies = [
        pltpu.make_async_copy(source, target, sems.at[number])
        for number, (source, target) in enumerate(
            ((nodes_hbm, nodes_ref), (leaves_hbm, leaves_ref), (moments_hbm, moments_ref))
        )
    ]
    for copy in copies:
        copy.start()
    for copy in copies:
        copy.wait()
    kept = reduce_rows(moments_ref[...])
    kept_ref[...] = kept
    table3 = jnp.concatenate(split(kept, 3), axis=0)
    own, peer_node, node_code = (nodes_ref[0, field] for field in range(3))
    leaf, peer_leaf, leaf_code = (leaves_ref[0, field] for field in range(3))
    fields = [
        own,
        jnp.where(own >= 0, peer_node, 0),
        jnp.where(own >= 0, node_code, 0),
        jnp.where(leaf >= 0, peer_leaf, -1),
        jnp.where(leaf >= 0, leaf_code, 0),
    ]
    stacked = jnp.concatenate([field.astype(F32) for field in fields], axis=0)
    source = lax.broadcasted_iota(I32, (128, 128), 0)
    target = lax.broadcasted_iota(I32, (128, 128), 1)
    lanes = jnp.where((source & 3) * 32 + (source >> 2) == target, 1.0, 0.0).astype(BF16)
    got = jnp.dot(jnp.concatenate(split(stacked, 2), axis=0), lanes, preferred_element_type=F32)
    moved = got[0:40] + got[40:80]
    block = lax.broadcasted_iota(I32, (128, 128), 0) >> 5 == (
        lax.broadcasted_iota(I32, (128, 128), 1) >> 5
    )
    row_number = lax.broadcasted_iota(I32, (8, 128), 0)
    for slab in range(8):
        rows = [moved[8 * field + slab : 8 * field + slab + 1] for field in range(5)]
        values = pick(table3, one_hot(rows[0].astype(I32), 256))
        last = values[24:32]
        for field, lane in ((0, OWN_NODE), (1, PEER_NODE), (2, NODE_CODE), (3, PEER_LEAF), (4, LEAF_CODE)):
            last = jnp.where(row_number == lane - 24, rows[field], last)
        values = jnp.concatenate([values[0:24], last], axis=0)
        turned = jnp.where(block, jnp.concatenate([values] * 4, axis=0), 0.0).T
        sent_ref[32 * slab : 32 * slab + 32, :] = (
            turned[0:32] + turned[32:64] + turned[64:96] + turned[96:128]
        )


def answer_kernel(
    links_ref, counts_ref, got_ref, kept_ref, positions_ref, masses_ref,
    reply_ref, partial_ref, asked_ref, cells_ref,
    turned, far_side, near_out, far_out, whole, rows, sems,
):
    whole[...] = got_ref[...].astype(I32)
    copies = []
    peers = [peer_of(shift) for shift in SHIFTS] + [peer_of(-shift) for shift in SHIFTS]
    for number in range(12):
        first = pl.multiple_of((peers[number] >> 3) * 8, 8)
        copies.append(
            pltpu.make_async_copy(whole.at[pl.ds(first, 8)], rows.at[number], sems.at[number])
        )
        copies[-1].start()
    for half in range(2):
        turned[128 * half : 128 * half + 128, :] = got_ref[128 * half : 128 * half + 128, :].T
    table3 = jnp.concatenate(split(kept_ref[...], 3), axis=0)
    for group in range(8):
        row = turned[32 * group + PEER_NODE : 32 * group + PEER_NODE + 1, :].astype(I32)
        far_side[32 * group : 32 * group + 32, :] = pick(table3, one_hot(row, 256))

    def store_near(number, value):
        near_out[pl.ds(number, 8, stride=32), :] = value

    def store_far(number, value):
        far_out[pl.ds(number, 8, stride=32), :] = value

    for number in range(RANK, 32):
        store_near(number, jnp.zeros((8, 128), F32))
        store_far(number, jnp.zeros((8, 128), F32))
    node_sums(
        strided(turned, 0, NODE_CODE).astype(I32),
        functools.partial(strided, turned, 0),
        functools.partial(strided, far_side, 0),
        store_near,
        store_far,
    )
    for half in range(2):
        reply_ref[128 * half : 128 * half + 128, :] = near_out[128 * half : 128 * half + 128, :].T
    total = jnp.zeros((32, 256), F32)
    for group in range(8):
        row = turned[32 * group + PEER_NODE : 32 * group + PEER_NODE + 1, :].astype(I32)
        total = total + put(far_out[32 * group : 32 * group + 32, :], one_hot(row, 256))
    partial_ref[...] = total
    for copy in copies:
        copy.wait()
    lane = lax.broadcasted_iota(I32, (1, 128), 1)

    def fill(number, slot, leaf):
        live = jnp.where(leaf >= 0, counts_ref[jnp.maximum(leaf, 0)], 0)
        leaf = jnp.maximum(leaf, 0)
        for axis in range(3):
            cells_ref[number, 4 * slot + axis : 4 * slot + axis + 1, :] = positions_ref[axis, pl.ds(leaf, 1), :]
        cells_ref[number, 4 * slot + 3 : 4 * slot + 4, :] = jnp.where(
            lane < live, masses_ref[pl.ds(leaf, 1), :], 0.0
        )

    for number in range(12):
        peer = peers[number]
        for slot in range(4):
            asked = rows[number, peer & 7, 32 * slot + PEER_LEAF]
            if number < 6:
                fill(number, slot, links_ref[0, 0, peer >> 5, (peer & 31) * 4 + slot])
                fill(number, 4 + slot, asked)
            else:
                asked_ref[number - 6, 2 * slot] = asked
                asked_ref[number - 6, 2 * slot + 1] = rows[number, peer & 7, 32 * slot + LEAF_CODE]


def leaf_offset(code):
    first = (code * 57) >> 9
    second = (code * 171) >> 9
    third = code - second * 3
    second = second - first * 3
    return [(part - 1).astype(F32) for part in (first, second, third)]


def eight_pairs(fields, left, right, terms_a, terms_b, sums_a, sums_b, pulls_a, pulls_b):
    a, b = ([fields[8 * (base + axis) : 8 * (base + axis) + 8, :] for axis in range(3)] for base in (0, 4))
    mass_a, mass_b = fields[24:32, :], fields[56:64, :]
    one = jnp.ones((8, 128), F32)
    rows_a, rows_b = [], []
    for axis in range(3):
        a1, a2, a3 = [part.astype(F32) for part in split(a[axis], 3)]
        b1, b2, b3 = [part.astype(F32) for part in split(-2.0 * b[axis], 3)]
        rows_a += [a1, a1, a2, a2, a1, a3]
        rows_b += [b1, b2, b1, b2, b3, b1]
    rows_a += [part.astype(F32) for part in split(a[0] * a[0] + a[1] * a[1] + a[2] * a[2] + softening, 3)]
    rows_b += [one] * 3
    rows_a += [one] * 3
    rows_b += [part.astype(F32) for part in split(b[0] * b[0] + b[1] * b[1] + b[2] * b[2], 3)]
    for number in range(24):
        left[pl.ds(number, 8, stride=32), :] = rows_a[number]
        right[pl.ds(number, 8, stride=32), :] = rows_b[number]
    sides = [(a, mass_a, terms_a)] + ([(b, mass_b, terms_b)] if terms_b is not None else [])
    for place, mass, terms in sides:
        for number, value in enumerate([mass * place[0], mass * place[1], mass * place[2], mass]):
            high, low = split(value, 2)
            terms[pl.ds(number, 8, stride=8), :] = high.astype(F32)
            terms[pl.ds(number + 4, 8, stride=8), :] = low.astype(F32)
    blank = jnp.zeros((32, 128), BF16)
    for group in range(2):
        turned = left[128 * group : 128 * group + 128, :].T.astype(BF16)
        block = right[128 * group : 128 * group + 128, :].astype(BF16)
        for half in range(2):
            columns = []
            for pair in (2 * half, 2 * half + 1):
                parts = [blank] * 4
                parts[pair] = block[32 * pair : 32 * pair + 32, :]
                columns.append(jnp.concatenate(parts, axis=0))
            squared = jnp.dot(turned, jnp.concatenate(columns, axis=1), preferred_element_type=F32)
            inverse = lax.rsqrt(squared)
            weight = inverse * (inverse * inverse)
            high, low = split(weight, 2)
            base = 8 * (4 * group + 2 * half)
            use = terms_a[base : base + 16, :].astype(BF16)
            got = jnp.dot(
                jnp.concatenate([use, use], axis=1),
                jnp.concatenate([high, low], axis=0),
                preferred_element_type=F32,
            )
            sums_b[base : base + 8, :] = got[0:8, 0:128]
            sums_b[base + 8 : base + 16, :] = got[8:16, 128:256]
            if terms_b is not None:
                use = terms_b[base : base + 16, :].astype(BF16)
                both = jnp.concatenate(
                    [
                        jnp.concatenate([high[:, 0:128], low[:, 0:128]], axis=1),
                        jnp.concatenate([high[:, 128:256], low[:, 128:256]], axis=1),
                    ],
                    axis=0,
                )
                got = lax.dot_general(
                    jnp.concatenate([use, use], axis=1),
                    both,
                    (((1,), (1,)), ((), ())),
                    preferred_element_type=F32,
                )
                sums_a[base : base + 8, :] = got[0:8, 0:128]
                sums_a[base + 8 : base + 16, :] = got[8:16, 128:256]
    results = [(b, sums_b, pulls_b)] + ([(a, sums_a, pulls_a)] if terms_b is not None else [])
    for own, sums, pulls in results:
        moved = [
            sums[pl.ds(number, 8, stride=8), :] + sums[pl.ds(number + 4, 8, stride=8), :] for number in range(4)
        ]
        for axis in range(3):
            pulls[8 * axis : 8 * axis + 8, :] = moved[axis] - own[axis] * moved[3]


def clear_rows(*refs):
    for ref in refs:
        for number in range(24, 32):
            ref[pl.ds(number, 8, stride=32), :] = jnp.zeros((8, 128), F32)


def local_nodes_kernel(pairs_ref, kept_ref, partial_ref, near_side, far_side, near_out, far_out):
    table3 = jnp.concatenate(split(kept_ref[...], 3), axis=0)
    for number in range(RANK, 32):
        near_out[pl.ds(number, 8, stride=32), :] = jnp.zeros((8, 128), F32)
        far_out[pl.ds(number, 8, stride=32), :] = jnp.zeros((8, 128), F32)
    total = jnp.zeros((32, 256), F32)
    for batch in range(2):
        code_rows = []
        for group in range(8):
            lanes = slice(1024 * batch + 128 * group, 1024 * batch + 128 * group + 128)
            first, second = (one_hot(pairs_ref[0, field : field + 1, lanes], 256) for field in range(2))
            near_side[32 * group : 32 * group + 32, :] = pick(table3, first)
            far_side[32 * group : 32 * group + 32, :] = pick(table3, second)
            code_rows.append(pairs_ref[0, 2:3, lanes])

        def store_near(number, value):
            near_out[pl.ds(number, 8, stride=32), :] = value

        def store_far(number, value):
            far_out[pl.ds(number, 8, stride=32), :] = value

        node_sums(
            jnp.concatenate(code_rows, axis=0),
            functools.partial(strided, near_side, 0),
            functools.partial(strided, far_side, 0),
            store_near,
            store_far,
        )
        for group in range(8):
            lanes = slice(1024 * batch + 128 * group, 1024 * batch + 128 * group + 128)
            first, second = (one_hot(pairs_ref[0, field : field + 1, lanes], 256) for field in range(2))
            total = total + put(near_out[32 * group : 32 * group + 32, :], first)
            total = total + put(far_out[32 * group : 32 * group + 32, :], second)
    partial_ref[...] = total


CHAINS = 4
EARLY = 3


def gather_pairs(sets, first_place, counts_ref, leaf_pairs_ref, positions_ref, masses_ref):
    lane = lax.broadcasted_iota(I32, (1, 128), 1)
    for chain, work in enumerate(sets):
        fields = work[0]
        for pair in range(8):
            place = first_place + chain * 8 + pair
            leaf = [leaf_pairs_ref[0, field, place] for field in range(2)]
            offset = leaf_offset(leaf_pairs_ref[0, 2, place])
            for side, sign in ((0, -0.5), (1, 0.5)):
                live = counts_ref[leaf[side]]
                for axis in range(3):
                    row = 8 * (4 * side + axis) + pair
                    fields[row : row + 1, :] = positions_ref[axis, pl.ds(leaf[side], 1), :] + sign * offset[axis]
                row = 8 * (4 * side + 3) + pair
                fields[row : row + 1, :] = jnp.where(lane < live, masses_ref[pl.ds(leaf[side], 1), :], 0.0)


def scatter_pairs(pulls_of, first_place, counts_ref, leaf_pairs_ref, pull_ref):
    lane = lax.broadcasted_iota(I32, (1, 128), 1)
    for chain in range(CHAINS):
        for pair in range(8):
            place = first_place + chain * 8 + pair
            for side in range(2):
                leaf = leaf_pairs_ref[0, side, place]
                live = lane < counts_ref[leaf]
                for axis in range(3):
                    pull_ref[axis, pl.ds(leaf, 1), :] += jnp.where(
                        live, pulls_of(chain, side, 8 * axis + pair), 0.0
                    )


def local_leaves_kernel(counts_ref, leaf_pairs_ref, positions_ref, masses_ref, pull_ref, *scratch):
    pull_ref[...] = jnp.zeros_like(pull_ref)
    sets = [scratch[9 * chain : 9 * chain + 9] for chain in range(CHAINS)]
    for work in sets:
        clear_rows(work[1], work[2])

    def step(number, _):
        place = number * (8 * CHAINS)
        gather_pairs(sets, place, counts_ref, leaf_pairs_ref, positions_ref, masses_ref)
        for work in sets:
            eight_pairs(*work)
        scatter_pairs(
            lambda chain, side, row: sets[chain][7 + side][row : row + 1, :],
            place, counts_ref, leaf_pairs_ref, pull_ref,
        )
        return 0

    lax.fori_loop(0, EARLY, step, 0)


def late_leaves_kernel(counts_ref, leaf_pairs_ref, positions_ref, masses_ref, late_ref, *scratch):
    sets = [scratch[9 * chain : 9 * chain + 9] for chain in range(CHAINS)]
    for work in sets:
        clear_rows(work[1], work[2])
    gather_pairs(sets, EARLY * 8 * CHAINS, counts_ref, leaf_pairs_ref, positions_ref, masses_ref)
    for chain, work in enumerate(sets):
        eight_pairs(*work)
        for side in range(2):
            late_ref[chain, side] = work[7 + side][...]


def final_kernel(
    links_ref, asked_ref, counts_ref, sent_ref, reply_ref, cross_ref, local_ref,
    cells0, cells1, cells2, cells3, cells4, cells5, positions_ref, pull_ref, late_ref, leaf_pairs_ref,
    out_ref, forces_ref,
    turned, turned_reply, fields, left, right, terms_a, sums_b, pulls_b,
):
    for half in range(2):
        part = slice(128 * half, 128 * half + 128)
        turned[part, :] = sent_ref[part, :].T
        turned_reply[part, :] = reply_ref[part, :].T
    total = cross_ref[...] + local_ref[...]
    for group in range(8):
        row = turned[32 * group + OWN_NODE : 32 * group + OWN_NODE + 1, :].astype(I32)
        total = total + put(turned_reply[32 * group : 32 * group + 32, :], one_hot(row, 256))
    expand_rows(total, out_ref)
    forces_ref[...] = pull_ref[...]
    scatter_pairs(
        lambda chain, side, row: late_ref[chain, side, row : row + 1, :],
        EARLY * 8 * CHAINS, counts_ref, leaf_pairs_ref, forces_ref,
    )
    clear_rows(left, right)
    lane = lax.broadcasted_iota(I32, (1, 128), 1)
    for number, cells in enumerate((cells0, cells1, cells2, cells3, cells4, cells5)):
        peer = peer_of(-SHIFTS[number])
        owns, lives = [], []
        for pair in range(8):
            slot = pair % 4
            if pair < 4:
                place = (peer >> 5, (peer & 31) * 4 + slot)
                own, code = links_ref[0, 0, place[0], place[1]], links_ref[0, 2, place[0], place[1]]
                source, sign = 4 + slot, 0.5
            else:
                own, code = asked_ref[number, 2 * slot], asked_ref[number, 2 * slot + 1]
                source, sign = slot, -0.5
            alive = own >= 0
            own = jnp.maximum(own, 0)
            offset = leaf_offset(jnp.where(alive, code, 0))
            owns.append(own)
            lives.append(jnp.where(alive, counts_ref[own], 0))
            for axis in range(3):
                row = 8 * axis + pair
                fields[row : row + 1, :] = (
                    cells[4 * source + axis : 4 * source + axis + 1, :] + sign * offset[axis]
                )
                fields[32 + row : 33 + row, :] = positions_ref[axis, pl.ds(own, 1), :] - sign * offset[axis]
            fields[24 + pair : 25 + pair, :] = cells[4 * source + 3 : 4 * source + 4, :]
        eight_pairs(fields, left, right, terms_a, None, None, sums_b, None, pulls_b)
        for pair in range(8):
            live = lane < lives[pair]
            for axis in range(3):
                forces_ref[axis, pl.ds(owns[pair], 1), :] += jnp.where(
                    live, pulls_b[8 * axis + pair : 8 * axis + pair + 1, :], 0.0
                )


SMEM = pl.BlockSpec(memory_space=pltpu.SMEM)
VMEM = pl.BlockSpec(memory_space=pltpu.VMEM)
HBM = pl.BlockSpec(memory_space=pltpu.HBM)
PARAMS = pltpu.CompilerParams(vmem_limit_bytes=32 * 1024 * 1024)


def exchange(sent):
    return lax.all_to_all(
        sent.reshape(DOMAINS, 1, 128), ("dx", "dy"), split_axis=0, concat_axis=0, tiled=True
    ).reshape(DOMAINS, 128)


def on_device(moments, positions, masses, counts, node_links, leaf_links, node_local, leaf_local):
    shape = jax.ShapeDtypeStruct
    block = pltpu.VMEM((256, 128), F32)
    tiles, pulls = pltpu.VMEM((64, 128), F32), pltpu.VMEM((24, 128), F32)
    kept, sent = pl.pallas_call(
        pack_kernel,
        out_shape=(shape((32, 256), F32), shape((256, 128), F32)),
        in_specs=[HBM] * 3,
        out_specs=(VMEM, VMEM),
        scratch_shapes=[
            pltpu.VMEM(moments.shape, F32),
            pltpu.VMEM(node_links.shape, I32),
            pltpu.VMEM(leaf_links.shape, I32),
            pltpu.SemaphoreType.DMA((3,)),
        ],
        compiler_params=pltpu.CompilerParams(vmem_limit_bytes=56 * 1024 * 1024),
        name="pack",
    )(moments, node_links, leaf_links)
    got = exchange(sent)
    local_exp = pl.pallas_call(
        local_nodes_kernel,
        out_shape=shape((32, 256), F32),
        in_specs=[VMEM] * 2,
        out_specs=VMEM,
        scratch_shapes=[block] * 4,
        compiler_params=PARAMS,
        cost_estimate=pl.CostEstimate(flops=300_000_000, bytes_accessed=300_000, transcendentals=2048),
        name="local_nodes",
    )(node_local, kept)
    leaf_early, local_exp = lax.optimization_barrier((leaf_local, local_exp))
    pull = pl.pallas_call(
        local_leaves_kernel,
        out_shape=shape(positions.shape, F32),
        in_specs=[SMEM, SMEM, VMEM, VMEM],
        out_specs=VMEM,
        scratch_shapes=[tiles, block, block, tiles, tiles, tiles, tiles, pulls, pulls] * CHAINS,
        compiler_params=PARAMS,
        cost_estimate=pl.CostEstimate(flops=80_000_000, bytes_accessed=3_000_000, transcendentals=2_100_000),
        name="local_leaves",
    )(counts, leaf_early, positions, masses)
    got, pull = lax.optimization_barrier((got, pull))
    reply, cross, asked, cells = pl.pallas_call(
        answer_kernel,
        out_shape=(
            shape((256, 128), F32),
            shape((32, 256), F32),
            shape((6, 8), I32),
            shape((6, 32, 128), F32),
        ),
        in_specs=[SMEM, SMEM] + [VMEM] * 4,
        out_specs=(VMEM, VMEM, SMEM, VMEM),
        scratch_shapes=[block] * 4
        + [pltpu.VMEM((256, 128), I32), pltpu.SMEM((12, 8, 128), I32), pltpu.SemaphoreType.DMA((12,))],
        compiler_params=PARAMS,
        name="answer",
    )(leaf_links, counts, got, kept, positions, masses)
    back = exchange(reply)
    moved = [
        lax.ppermute(
            cells[number],
            ("dx", "dy"),
            [(device, (device + shift) % DOMAINS) for device in range(DOMAINS)],
        )
        for number, shift in enumerate(SHIFTS)
    ]
    leaf_pairs_late, moved[5] = lax.optimization_barrier((leaf_local, moved[5]))
    late = pl.pallas_call(
        late_leaves_kernel,
        out_shape=shape((CHAINS, 2, 24, 128), F32),
        in_specs=[SMEM, SMEM, VMEM, VMEM],
        out_specs=VMEM,
        scratch_shapes=[tiles, block, block, tiles, tiles, tiles, tiles, pulls, pulls] * CHAINS,
        compiler_params=PARAMS,
        cost_estimate=pl.CostEstimate(flops=20_000_000, bytes_accessed=1_500_000, transcendentals=500_000),
        name="late_leaves",
    )(counts, leaf_pairs_late, positions, masses)
    return pl.pallas_call(
        final_kernel,
        out_shape=(shape(moments.shape, F32), shape(positions.shape, F32)),
        in_specs=[SMEM] * 3 + [VMEM] * 13 + [SMEM],
        out_specs=(VMEM, VMEM),
        scratch_shapes=[block, block, tiles, block, block, tiles, tiles, pulls],
        compiler_params=PARAMS,
        name="final",
    )(leaf_links, asked, counts, sent, back, cross, local_exp, *moved, positions, pull, late, leaf_local)


def solution(mesh):
    in_specs = (
        P(None, ("dx", "dy")),
        P(None, ("dx", "dy"), None),
        P(("dx", "dy"), None),
        P(("dx", "dy")),
        P(("dx", "dy"), None, None, None),
        P(("dx", "dy"), None, None, None),
        P(("dx", "dy"), None, None),
        P(("dx", "dy"), None, None),
    )
    out_specs = (P(None, ("dx", "dy")), P(None, ("dx", "dy"), None))
    return jax.shard_map(
        on_device, mesh=mesh, in_specs=in_specs, out_specs=out_specs, check_vma=False
    )
```
